256 devices in a mesh: row: 8 (over z), col: 32 (over y, x, core).
Axes of the slice: x: 4, y: 4, z: 8, core: 2. Of those that a mesh axis runs over, the one named last changes fastest.
Arguments:
- transitions: bfloat16 [16384, 16384], P('row', 'col'), as said below
- forward: bfloat16 [2, 16384, 512], P(None, 'row'), may hold values from 0.02 to 3
- emission: bfloat16 [2, 16384, 512], P(None, ('row', 'col')), may hold values from 0.01 to 1
- beta_end: float32 [16384, 512], P(('row', 'col')), may hold values from 0.2 to 5
- token_ids: int32 [2, 512], replicated, may hold values from 0 to 50256, as said below
Outputs:
- counts: float32 [16384, 16384], P('row', 'col')
- beta_start: float32 [16384, 512], P(('row', 'col'))
- log_scales: float32 [2, 512], replicated
The draws below stay inside these ranges and needn't reach their ends.
Inputs may be any that keep to these rules, and one draw needn't show every extreme that they name: `token_ids`: the id 50257 - 1 marks a step past the end of the sequence; once a sequence has ended, every later step of it has that id. `transitions`: every entry is positive.
All inputs are finite; a program needn't handle non-finite values.
Results may differ from the reference program's by a relative error of at most 0.00033.
Values may be sent and summed in bfloat16 or wider, within the bound.
No kernel may reach another device: no remote copies, remote signals or barrier semaphores. Data moves between devices by JAX's collectives and lax.ppermute only.
A program may use at most 64 MiB of HBM per device.

```python
import math
import jax
import jax.numpy as jnp

STATES = 16384
VOCAB = 50257
SEQS = 512
STEPS = 2
PIECE = 64
SRC_BLOCK = 2048
DST_BLOCK = 512
N_ROW = 8
N_COL = 32


def state_group(key):
    return jax.random.randint(jax.random.fold_in(key, 7), (STATES,), 0, 3) == 0


def state_factor(key):
    return jnp.exp(jax.random.uniform(jax.random.fold_in(key, 13), (STATES,), jnp.float32, -1.0, 1.0))


def destination_state():
    position = jnp.arange(STATES, dtype=jnp.int32)
    dest_block = position // DST_BLOCK
    in_block = position % DST_BLOCK
    return (in_block // PIECE * SRC_BLOCK + dest_block * PIECE + position % PIECE).astype(jnp.int32)


def draw_transitions(key, part):
    normal_draw = jax.random.normal(key, (STATES, STATES), jnp.float32)
    base = jnp.exp(2.5 * jnp.clip(normal_draw, -3.0, 3.0)) / 83.0
    group = state_group(key)
    factor = state_factor(key)
    dest_state = destination_state()
    affinity = jnp.where(group[:, None] == group[dest_state][None, :], jnp.float32(4.0), jnp.float32(1.0))
    return (base * factor[:, None] * factor[dest_state][None, :] * affinity).astype(jnp.bfloat16)


def draw_forward(key, part):
    group = state_group(key)
    fresh = jax.random.uniform(jax.random.fold_in(key, 31), (STEPS, STATES, SEQS), jnp.float32)
    base = jnp.where(group[None, :, None], 0.3 * jnp.exp(2.302585 * fresh), 0.1 * jnp.exp(2.302585 * fresh))
    level = jnp.exp(jax.random.uniform(jax.random.fold_in(key, 37), (STEPS, 1, SEQS), jnp.float32, -1.6, 0.0))
    return (base * level).astype(jnp.bfloat16)


def draw_emission(key, part):
    group = state_group(key)
    fresh = jax.random.uniform(jax.random.fold_in(key, 41), (STEPS, STATES, SEQS), jnp.float32)
    base = jnp.where(group[None, :, None], 0.1 * jnp.exp(2.302585 * fresh), 0.01 * jnp.exp(2.302585 * fresh))
    return base.astype(jnp.bfloat16)


def draw_token_ids(key, part):
    key_words = jax.random.fold_in(key, 11)
    key_length = jax.random.fold_in(key, 23)
    words = jax.random.randint(key_words, (STEPS, SEQS), 0, VOCAB - 1)
    length = jax.random.randint(key_length, (SEQS,), 0, 2 * STEPS + 1)
    length = length.at[0].set(0)
    steps_here = jnp.arange(STEPS, dtype=jnp.int32)[:, None]
    return jnp.where(steps_here >= length[None, :], VOCAB - 1, words).astype(jnp.int32)


def block_scale(stream_key, shape, split, least, largest):
    def one(axis_at, blocks):
        heights = jax.random.uniform(jax.random.fold_in(jax.random.fold_in(stream_key, 6), axis_at), (blocks,), jnp.float32, least / len(split), largest / len(split))
        return jnp.repeat(jnp.exp(heights), shape[axis_at] // blocks).reshape((-1,) + (1,) * (len(shape) - axis_at - 1))

    gain = one(*split[0])
    for cut in split[1:]:
        gain = gain * one(*cut)
    return gain


def setup_inputs(seed: int = 0) -> dict:
    arg_keys = jax.random.split(jax.random.key(seed), 6)
    return {
        "transitions": draw_transitions(jax.random.fold_in(arg_keys[5], 71), 0),
        "forward": draw_forward(jax.random.fold_in(arg_keys[5], 71), 0),
        "emission": draw_emission(jax.random.fold_in(arg_keys[5], 71), 0),
        "beta_end": jnp.clip(jnp.exp(math.log(5.0) - 3.218876 * jax.random.uniform(arg_keys[3], (STATES, SEQS), jnp.float32) ** block_scale(arg_keys[3], (STATES, SEQS), ((0, 256),), -0.2, 0.2)), 0.2, 5.0),
        "token_ids": draw_token_ids(jax.random.fold_in(arg_keys[5], 71), 0),
    }


def column_order(field):
    return field.reshape(N_ROW, N_COL, PIECE, SEQS).transpose(1, 0, 2, 3).reshape(STATES, SEQS)


def reference(transitions, forward, emission, beta_end, token_ids):
    beta = beta_end
    post_list = []
    weight_list = []
    log_list = [None] * STEPS
    for step in reversed(range(STEPS)):
        ended = token_ids[step] == VOCAB - 1
        observed = jnp.where(ended[None, :], jnp.float32(1.0), emission[step].astype(jnp.float32))
        weights = (observed * beta).astype(jnp.bfloat16)
        weights_col = column_order(weights)
        raw = jnp.zeros((STATES, SEQS), jnp.float32)
        for block in range(N_COL):
            cols = transitions[:, block * DST_BLOCK:(block + 1) * DST_BLOCK]
            part = jnp.dot(cols, weights_col[block * DST_BLOCK:(block + 1) * DST_BLOCK], preferred_element_type=jnp.float32) / STATES
            raw = raw + part
        scale = jnp.mean(raw, axis=0)
        alpha = forward[step].astype(jnp.float32)
        norm = jnp.mean(alpha * raw, axis=0)
        post_list.append((alpha / norm[None, :]).astype(jnp.bfloat16))
        weight_list.append(weights_col)
        log_list[step] = jnp.log(scale)
        beta = raw / scale[None, :]
    posts = jnp.concatenate(post_list, axis=1)
    wcols = jnp.concatenate(weight_list, axis=1)
    mixed = jnp.dot(posts, wcols.T, preferred_element_type=jnp.float32)
    counts = transitions.astype(jnp.float32) * mixed / SEQS
    return counts, beta, jnp.stack(log_list)
```

```python
import jax
import jax.numpy as jnp
from jax import lax
from jax.sharding import Mesh, PartitionSpec as P

VOCAB = 50257
COL = ("y", "x", "core")
CHIPS = ("y", "x")
BF16 = jnp.bfloat16
F16 = jnp.float16
F32 = jnp.float32


def split3(v):
    hi = lax.reduce_precision(v, 8, 7)
    mid = lax.reduce_precision(v - hi, 8, 7)
    return [part.astype(BF16) for part in (hi, mid, v - hi - mid)]


def split2(v):
    hi = lax.reduce_precision(v, 5, 10)
    return [hi.astype(F16), (v - hi).astype(F16)]


def rows8(rows):
    block = jnp.stack(rows)
    return jnp.pad(block, ((0, 8 - block.shape[0]), (0, 0)))


def local(transitions, forward, emission, beta_end, token_ids):
    src, dst = transitions.shape
    piece, seqs = beta_end.shape
    n_row = lax.axis_size("row")
    n_chip = lax.axis_size("y") * lax.axis_size("x")
    n_core = lax.axis_size("core")
    states = float(dst * n_chip * n_core)
    core = lax.axis_index("core")
    swap = [(i, (i + 1) % n_core) for i in range(n_core)]

    def observed(step):
        ended = token_ids[step] == VOCAB - 1
        return jnp.where(ended[None, :], F32(1.0), emission[step].astype(F32))

    def gather(weights, extra):
        block = jnp.concatenate([weights, rows8(extra)], axis=0)
        block = jnp.broadcast_to(block[None], (n_row,) + block.shape)
        return lax.all_to_all(block, "row", 0, 0)

    def body(block):
        return block[:, :piece].reshape(n_row * piece, seqs)

    def extras(block, i):
        return jnp.sum(block[:, piece + i:piece + i + 3].astype(F32), axis=(0, 1))

    chunks = transitions.reshape(n_chip, n_core, piece, dst)
    half = n_chip * piece
    mine = lax.dynamic_index_in_dim(chunks, core, 1, keepdims=False).reshape(half, dst)
    theirs = lax.dynamic_index_in_dim(chunks, 1 - core, 1, keepdims=False).reshape(half, dst)
    t_other = lax.ppermute(theirs, "core", swap)
    fwd = lax.dynamic_index_in_dim(
        forward.reshape(2, n_chip, n_core, piece, seqs), core, 2, keepdims=False
    ).reshape(2, half, seqs)

    g_part = lax.dot_general(
        transitions, forward[0], (((0,), (0,)), ((), ())), preferred_element_type=F32
    )
    g_own = lax.psum_scatter(g_part, "row", scatter_dimension=0, tiled=True)

    def backward(block, other, cs_own, cs_other, norm_chip, step):
        w_own, w_other = body(block), body(other)
        sc = jnp.dot(cs_own, w_own, preferred_element_type=F32)
        sc = sc + jnp.dot(cs_other, w_other, preferred_element_type=F32)
        sc = jnp.sum(sc, axis=0) / states / states
        part = jnp.dot(mine, w_own, preferred_element_type=F32)
        part = part + jnp.dot(t_other, w_other, preferred_element_type=F32)
        part = part / states
        if norm_chip is None:
            norm_chip = jnp.sum(fwd[step].astype(F32) * part, axis=0) / states
        power = jnp.ceil(jnp.log2(sc))
        down = jnp.exp2(-power)
        data = (part * down[None, :]).astype(F16).reshape(n_chip, piece, seqs)
        extra = rows8([power.astype(F16)] + split2(sc * down) + split2(norm_chip * down))
        extra = jnp.broadcast_to(extra[None], (n_chip,) + extra.shape)
        got = lax.all_to_all(jnp.concatenate([data, extra], axis=1), CHIPS, 0, 0).astype(F32)
        up = jnp.exp2(got[:, piece:piece + 1])
        raw = jnp.sum(got[:, :piece] * up, axis=0)
        scale = jnp.sum(got[:, piece + 1:piece + 3] * up, axis=(0, 1))
        norm = jnp.sum(got[:, piece + 3:piece + 5] * up, axis=(0, 1))
        return w_own, raw, scale, norm

    weights = (observed(1) * beta_end).astype(BF16)
    colsum = jnp.sum(transitions.astype(F32), axis=0)
    block = gather(weights, split3(colsum))
    other = lax.ppermute(block, "core", swap)
    cs_own = jnp.stack(split3(extras(block, 0)))
    cs_other = jnp.stack(split3(extras(other, 0)))
    w1, raw, scale1, norm1_part = backward(block, other, cs_own, cs_other, None, 1)

    weights = (observed(0) * (raw / scale1[None, :])).astype(BF16)
    norm0_part = jnp.sum(weights.astype(F32) * g_own, axis=0) / states / states
    block = gather(weights, split3(norm1_part) + split3(norm0_part))
    other = lax.ppermute(block, "core", swap)
    norm1 = extras(block, 0) + extras(other, 0)
    norm0_chip = extras(block, 3) + extras(other, 3)
    w0, raw, scale0, norm0 = backward(block, other, cs_own, cs_other, norm0_chip, 0)
    beta = raw / scale0[None, :]

    post1 = (forward[1].astype(F32) / norm1[None, :]).astype(BF16)
    post0 = (forward[0].astype(F32) / norm0[None, :]).astype(BF16)
    mixed = lax.dot_general(post1, w1, (((1,), (1,)), ((), ())), preferred_element_type=F32)
    mixed = mixed + lax.dot_general(post0, w0, (((1,), (1,)), ((), ())), preferred_element_type=F32)
    counts = transitions.astype(F32) * mixed / seqs
    return counts, beta, jnp.stack([jnp.log(scale0), jnp.log(scale1)])


def solution(mesh):
    n_row, n_col = mesh.devices.shape
    grid = Mesh(mesh.devices.reshape(n_row, 4, n_col // 8, 2), ("row",) + COL)
    in_specs = (
        P("row", COL),
        P(None, "row", None),
        P(None, ("row",) + COL, None),
        P(("row",) + COL, None),
        P(),
    )
    out_specs = (P("row", COL), P(("row",) + COL, None), P())
    return jax.shard_map(local, mesh=grid, in_specs=in_specs, out_specs=out_specs, check_vma=False)
```

```python
import jax
import jax.numpy as jnp
from jax import lax
from jax.experimental import pallas as pl
from jax.experimental.pallas import tpu as pltpu
from jax.sharding import Mesh, PartitionSpec as P

VOCAB = 50257
COL = ("y", "x", "core")
CHIPS = ("y", "x")
BF16 = jnp.bfloat16
F16 = jnp.float16
F32 = jnp.float32
EXTRA = 8
TILE = 256
CHUNK = 512
NT = (((1,), (1,)), ((), ()))
TN = (((0,), (0,)), ((), ()))
WHOLE = pl.BlockSpec(memory_space=pltpu.VMEM)


def params(mib):
    return pltpu.CompilerParams(vmem_limit_bytes=mib * 1024 * 1024)


def split3(v):
    hi = lax.reduce_precision(v, 8, 7)
    mid = lax.reduce_precision(v - hi, 8, 7)
    return [part.astype(BF16) for part in (hi, mid, v - hi - mid)]


def split2(v):
    hi = lax.reduce_precision(v, 5, 10)
    return [hi, lax.reduce_precision(v - hi, 5, 10)]


def rows8(rows):
    block = jnp.stack(rows)
    return jnp.pad(block, ((0, EXTRA - block.shape[0]), (0, 0)))


def start_kernel(at_ref, t_hbm, f_hbm, e_hbm, b_hbm, tok_hbm, pay_ref, mine_ref, alpha_ref, seen_ref,
                 t_ref, f_ref, a_ref, e_ref, b_ref, tok_ref, g_ref, sems):
    core, col = at_ref[0], at_ref[1]
    piece = b_ref.shape[0]
    src = t_ref.shape[0]
    parts = src // CHUNK

    def copy(source, target, i):
        c = pltpu.make_async_copy(source, target, sems.at[i])
        c.start()
        return c

    loads = []
    for i in range(parts):
        rows = pl.ds(i * CHUNK, CHUNK)
        loads.append((
            copy(t_hbm.at[rows, :], t_ref.at[rows, :], 2 * i),
            copy(f_hbm.at[0, rows, :], f_ref.at[rows, :], 2 * i + 1),
        ))
    own = pl.ds(pl.multiple_of(col * piece, piece), piece)
    small = [
        copy(f_hbm.at[1, own, :], a_ref, 2 * parts),
        copy(e_hbm, e_ref, 2 * parts + 1),
        copy(b_hbm, b_ref, 2 * parts + 2),
        copy(tok_hbm, tok_ref, 2 * parts + 3),
    ]
    ones = jnp.ones((EXTRA, CHUNK), BF16)
    sums = jnp.zeros((EXTRA, t_ref.shape[1]), F32)
    for i in range(parts):
        for c in loads[i]:
            c.wait()
        t = t_ref[i * CHUNK:(i + 1) * CHUNK, :]
        f = f_ref[i * CHUNK:(i + 1) * CHUNK, :]
        g = lax.dot_general(t, f, TN, preferred_element_type=F32)
        if i == 0:
            g_ref[...] = g
        else:
            g_ref[...] += g
        sums = sums + jnp.dot(ones, t, preferred_element_type=F32)
    for i in range(src // (2 * piece)):
        rows = pl.ds(pl.multiple_of((2 * i + core) * piece, piece), piece)
        mine_ref[i * piece:(i + 1) * piece, :] = t_ref[rows, :]
    for c in small:
        c.wait()
    alpha_ref[...] = a_ref[...].astype(F32)
    ended = tok_ref[...] == VOCAB - 1
    seen_ref[...] = jnp.where(ended[0:1], F32(1.0), e_ref[0].astype(F32))
    observed = jnp.where(ended[1:2], F32(1.0), e_ref[1].astype(F32))
    weights = (observed * b_ref[...]).astype(BF16)
    hi = sums.astype(BF16).astype(F32)
    mid = (sums - hi).astype(BF16).astype(F32)
    lo = sums - hi - mid
    row = lax.broadcasted_iota(jnp.int32, sums.shape, 0)
    tail = jnp.where(row == 0, hi, jnp.where(row == 1, mid, jnp.where(row == 2, lo, F32(0.0))))
    tail = tail.astype(BF16)
    for r in range(pay_ref.shape[0]):
        part = g_ref[r * piece:(r + 1) * piece, :].astype(BF16)
        pay_ref[r] = jnp.concatenate([weights, part, tail], axis=0)


def start_call(at, transitions, forward, emission, beta_end, token_ids, n_row):
    src, dst = transitions.shape
    piece, seqs = beta_end.shape
    return pl.pallas_call(
        start_kernel,
        out_shape=(
            jax.ShapeDtypeStruct((n_row, 2 * piece + EXTRA, seqs), BF16),
            jax.ShapeDtypeStruct((src // 2, dst), BF16),
            jax.ShapeDtypeStruct((piece, seqs), F32),
            jax.ShapeDtypeStruct((piece, seqs), F32),
        ),
        in_specs=[pl.BlockSpec(memory_space=pltpu.SMEM)] + [pl.BlockSpec(memory_space=pl.ANY)] * 5,
        out_specs=(WHOLE,) * 4,
        scratch_shapes=[
            pltpu.VMEM((src, dst), BF16),
            pltpu.VMEM((src, seqs), BF16),
            pltpu.VMEM((piece, seqs), BF16),
            pltpu.VMEM(emission.shape, BF16),
            pltpu.VMEM((piece, seqs), F32),
            pltpu.VMEM(token_ids.shape, jnp.int32),
            pltpu.VMEM((dst, seqs), F32),
            pltpu.SemaphoreType.DMA((2 * (src // CHUNK) + 4,)),
        ],
        compiler_params=params(56),
    )(at, transitions, forward, emission, beta_end, token_ids)


def product_kernel(mine_ref, other_ref, w_ref, v_ref, mul_ref, extra_ref, out_ref):
    n_chip, rows, _ = out_ref.shape
    piece = rows - EXTRA
    mul = mul_ref[...]
    extra = extra_ref[...]
    group = TILE // piece
    for i in range(n_chip // group):
        at = pl.ds(i * TILE, TILE)
        part = jnp.dot(mine_ref[at, :], w_ref[...], preferred_element_type=F32)
        part = part + jnp.dot(other_ref[at, :], v_ref[...], preferred_element_type=F32)
        part = part * mul
        for j in range(group):
            out_ref[i * group + j, :piece, :] = part[j * piece:(j + 1) * piece]
            out_ref[i * group + j, piece:, :] = extra


def counts_kernel(t_hbm, f_hbm, w1_ref, w0_ref, raw_ref, sums_ref, out_hbm, beta_ref, log_ref,
                  t_ref, f_ref, o_ref, w1t_ref, w0t_ref, sems):
    src, seqs = f_ref.shape[1:]
    parts = src // TILE
    loads, stores = [], []
    for i in range(parts):
        rows = pl.ds(i * TILE, TILE)
        loads.append((
            pltpu.make_async_copy(t_hbm.at[rows, :], t_ref.at[rows, :], sems.at[3 * i]),
            pltpu.make_async_copy(f_hbm.at[:, rows, :], f_ref.at[:, rows, :], sems.at[3 * i + 1]),
        ))
        stores.append(pltpu.make_async_copy(o_ref.at[rows, :], out_hbm.at[rows, :], sems.at[3 * i + 2]))
        for c in loads[i]:
            c.start()
    w1t_ref[...] = w1_ref[...].T
    w0t_ref[...] = w0_ref[...].T
    beta_ref[...] = raw_ref[...] / sums_ref[2:3, :]
    log_ref[...] = jnp.log(sums_ref[2:4, :])
    inv = 1.0 / sums_ref[0:2, :]
    for i in range(parts):
        for c in loads[i]:
            c.wait()
        at = slice(i * TILE, (i + 1) * TILE)
        post1 = (f_ref[1, at, :].astype(F32) * inv[1:2]).astype(BF16)
        post0 = (f_ref[0, at, :].astype(F32) * inv[0:1]).astype(BF16)
        mixed = jnp.dot(post1, w1t_ref[...], preferred_element_type=F32)
        mixed = mixed + jnp.dot(post0, w0t_ref[...], preferred_element_type=F32)
        o_ref[at, :] = t_ref[at, :].astype(F32) * (mixed * (1.0 / seqs))
        stores[i].start()
    for c in stores:
        c.wait()


def counts_call(transitions, forward, w1, w0, raw, sums):
    src, dst = transitions.shape
    steps, _, seqs = forward.shape
    return pl.pallas_call(
        counts_kernel,
        out_shape=(
            jax.ShapeDtypeStruct((src, dst), F32),
            jax.ShapeDtypeStruct(raw.shape, F32),
            jax.ShapeDtypeStruct((steps, seqs), F32),
        ),
        in_specs=[pl.BlockSpec(memory_space=pl.ANY)] * 2 + [WHOLE] * 4,
        out_specs=(pl.BlockSpec(memory_space=pl.ANY), WHOLE, WHOLE),
        scratch_shapes=[
            pltpu.VMEM((src, dst), BF16),
            pltpu.VMEM((steps, src, seqs), BF16),
            pltpu.VMEM((src, dst), F32),
            pltpu.VMEM((seqs, dst), BF16),
            pltpu.VMEM((seqs, dst), BF16),
            pltpu.SemaphoreType.DMA((3 * (src // TILE),)),
        ],
        compiler_params=params(56),
    )(transitions, forward, w1, w0, raw, sums)


def local(transitions, forward, emission, beta_end, token_ids):
    src, dst = transitions.shape
    piece, seqs = beta_end.shape
    n_row = lax.axis_size("row")
    n_chip = lax.axis_size("y") * lax.axis_size("x")
    n_core = lax.axis_size("core")
    states = float(dst * n_chip * n_core)
    core = lax.axis_index("core")
    col = (lax.axis_index("y") * lax.axis_size("x") + lax.axis_index("x")) * n_core + core
    swap = [(i, (i + 1) % n_core) for i in range(n_core)]

    chunks = transitions.reshape(n_chip, n_core, piece, dst)
    theirs = lax.dynamic_index_in_dim(chunks, 1 - core, 1, keepdims=False).reshape(src // 2, dst)
    t_other = lax.ppermute(theirs, "core", swap)
    at = jnp.stack([core, col]).astype(jnp.int32)
    pay, mine, alpha, observed = start_call(
        at, transitions, forward, emission, beta_end, token_ids, n_row
    )
    pay, mine, t_other = lax.optimization_barrier((pay, mine, t_other))

    block = lax.all_to_all(pay, "row", 0, 0)
    w1 = block[:, :piece].reshape(dst, seqs)
    g_own = jnp.sum(block[:, piece:2 * piece].astype(F32), axis=0)
    cs = jnp.sum(block[:, 2 * piece:2 * piece + 3].astype(F32), axis=(0, 1))
    cs = jnp.stack(split3(cs))

    def backward(w_own, totals):
        w_other = lax.ppermute(w_own, "core", swap)
        sc = jnp.sum(jnp.dot(cs, w_own, preferred_element_type=F32), axis=0) / states / states
        own = jnp.stack([sc] + totals)
        both = own + lax.ppermute(own, "core", swap)
        power = jnp.ceil(jnp.log2(both[0]))
        down = jnp.exp2(-power)
        rows = [power]
        for i in range(both.shape[0]):
            rows += split2(both[i] * down)
        data = pl.pallas_call(
            product_kernel,
            out_shape=jax.ShapeDtypeStruct((n_chip, piece + EXTRA, seqs), F32),
            in_specs=[WHOLE] * 6,
            out_specs=WHOLE,
            compiler_params=params(16),
        )(mine, t_other, w_own, w_other, (down / states)[None, :], rows8(rows))
        return data.astype(F16), both.shape[0]

    def collect(data, n):
        got = lax.all_to_all(data, CHIPS, 0, 0).astype(F32)
        up = jnp.exp2(got[:, piece:piece + 1])
        raw = jnp.sum(got[:, :piece] * up, axis=0)
        sums = jnp.sum(got[:, piece + 1:] * up, axis=0)
        return raw, [sums[2 * i] + sums[2 * i + 1] for i in range(n)]

    data, n = backward(w1, [])
    data, g_own = lax.optimization_barrier((data, g_own))
    raw, (scale1,) = collect(data, n)

    weights = (observed * (raw / scale1[None, :])).astype(BF16)
    norm1 = jnp.sum(alpha * raw, axis=0) / states
    norm0 = jnp.sum(weights.astype(F32) * g_own, axis=0) / states / states
    pay = jnp.concatenate([weights, rows8(split3(norm1) + split3(norm0))], axis=0)
    block = lax.all_to_all(jnp.broadcast_to(pay[None], (n_row,) + pay.shape), "row", 0, 0)
    w0 = block[:, :piece].reshape(dst, seqs)
    sums = jnp.sum(block[:, piece:].astype(F32), axis=0)
    norm1 = sums[0] + sums[1] + sums[2]
    norm0 = sums[3] + sums[4] + sums[5]
    data, n = backward(w0, [norm1, norm0])
    raw, (scale0, norm1, norm0) = collect(data, n)

    sums = rows8([norm0, norm1, scale0, scale1])
    return counts_call(transitions, forward, w1, w0, raw, sums)


def solution(mesh):
    n_row, n_col = mesh.devices.shape
    grid = Mesh(mesh.devices.reshape(n_row, 4, n_col // 8, 2), ("row",) + COL)
    in_specs = (
        P("row", COL),
        P(None, "row", None),
        P(None, ("row",) + COL, None),
        P(("row",) + COL, None),
        P(),
    )
    out_specs = (P("row", COL), P(("row",) + COL, None), P())
    return jax.shard_map(local, mesh=grid, in_specs=in_specs, out_specs=out_specs, check_vma=False)
```

```python
import jax
import jax.numpy as jnp
from jax import lax
from jax.experimental import pallas as pl
from jax.experimental.pallas import tpu as pltpu
from jax.sharding import Mesh, PartitionSpec as P

VOCAB = 50257
COL = ("y", "x", "core")
CHIPS = ("y", "x")
BF16 = jnp.bfloat16
F16 = jnp.float16
F32 = jnp.float32
EXTRA = 8
TILE = 256
CHUNK = 512
START = 50
COUNTS = 52
ANY = pl.BlockSpec(memory_space=pl.ANY)
TN = (((0,), (0,)), ((), ()))
WHOLE = pl.BlockSpec(memory_space=pltpu.VMEM)


def params(mib):
    return pltpu.CompilerParams(vmem_limit_bytes=mib * 1024 * 1024)


def split3(v):
    hi = lax.reduce_precision(v, 8, 7)
    mid = lax.reduce_precision(v - hi, 8, 7)
    return [part.astype(BF16) for part in (hi, mid, v - hi - mid)]


def split2(v):
    hi = lax.reduce_precision(v, 5, 10)
    return [hi, lax.reduce_precision(v - hi, 5, 10)]


def rows8(rows):
    block = jnp.stack(rows)
    return jnp.pad(block, ((0, EXTRA - block.shape[0]), (0, 0)))


def column():
    core = lax.axis_index("core")
    chip = lax.axis_index("y") * lax.axis_size("x") + lax.axis_index("x")
    return core, chip * lax.axis_size("core") + core


def start_kernel(t_hbm, f_hbm, e_hbm, b_hbm, tok_hbm, pay_ref, mine_ref, alpha_ref, seen_ref,
                 t_ref, f_ref, a_ref, e_ref, b_ref, tok_ref, g_ref, sems):
    core, col = column()
    piece = b_ref.shape[0]
    src = t_ref.shape[0]
    parts = src // CHUNK

    def copy(source, target, i):
        c = pltpu.make_async_copy(source, target, sems.at[i])
        c.start()
        return c

    loads = []
    for i in range(parts):
        rows = pl.ds(i * CHUNK, CHUNK)
        loads.append((
            copy(t_hbm.at[rows, :], t_ref.at[rows, :], 2 * i),
            copy(f_hbm.at[0, rows, :], f_ref.at[rows, :], 2 * i + 1),
        ))
    own = pl.ds(pl.multiple_of(col * piece, piece), piece)
    small = [
        copy(f_hbm.at[1, own, :], a_ref, 2 * parts),
        copy(e_hbm, e_ref, 2 * parts + 1),
        copy(b_hbm, b_ref, 2 * parts + 2),
        copy(tok_hbm, tok_ref, 2 * parts + 3),
    ]
    ones = jnp.ones((EXTRA, CHUNK), BF16)
    sums = jnp.zeros((EXTRA, t_ref.shape[1]), F32)
    for i in range(parts):
        for c in loads[i]:
            c.wait()
        t = t_ref[i * CHUNK:(i + 1) * CHUNK, :]
        f = f_ref[i * CHUNK:(i + 1) * CHUNK, :]
        g = lax.dot_general(t, f, TN, preferred_element_type=F32)
        if i == 0:
            g_ref[...] = g
        else:
            g_ref[...] += g
        sums = sums + jnp.dot(ones, t, preferred_element_type=F32)
    for i in range(src // (2 * piece)):
        rows = pl.ds(pl.multiple_of((2 * i + core) * piece, piece), piece)
        mine_ref[i * piece:(i + 1) * piece, :] = t_ref[rows, :]
    for c in small:
        c.wait()
    alpha_ref[...] = a_ref[...].astype(F32)
    ended = tok_ref[...] == VOCAB - 1
    seen_ref[...] = jnp.where(ended[0:1], F32(1.0), e_ref[0].astype(F32))
    observed = jnp.where(ended[1:2], F32(1.0), e_ref[1].astype(F32))
    weights = (observed * b_ref[...]).astype(BF16)
    hi = sums.astype(BF16).astype(F32)
    mid = (sums - hi).astype(BF16).astype(F32)
    lo = sums - hi - mid
    row = lax.broadcasted_iota(jnp.int32, sums.shape, 0)
    tail = jnp.where(row == 0, hi, jnp.where(row == 1, mid, jnp.where(row == 2, lo, F32(0.0))))
    tail = tail.astype(BF16)
    for r in range(pay_ref.shape[0]):
        part = g_ref[r * piece:(r + 1) * piece, :].astype(BF16)
        pay_ref[r] = jnp.concatenate([weights, part, tail], axis=0)


def start_call(transitions, forward, emission, beta_end, token_ids, n_row):
    src, dst = transitions.shape
    piece, seqs = beta_end.shape
    return pl.pallas_call(
        start_kernel,
        out_shape=(
            jax.ShapeDtypeStruct((n_row, 2 * piece + EXTRA, seqs), BF16),
            jax.ShapeDtypeStruct((src // 2, dst), BF16),
            jax.ShapeDtypeStruct((piece, seqs), F32),
            jax.ShapeDtypeStruct((piece, seqs), F32),
        ),
        in_specs=[pl.BlockSpec(memory_space=pl.ANY)] * 5,
        out_specs=(WHOLE,) * 4,
        scratch_shapes=[
            pltpu.VMEM((src, dst), BF16),
            pltpu.VMEM((src, seqs), BF16),
            pltpu.VMEM((piece, seqs), BF16),
            pltpu.VMEM(emission.shape, BF16),
            pltpu.VMEM((piece, seqs), F32),
            pltpu.VMEM(token_ids.shape, jnp.int32),
            pltpu.VMEM((dst, seqs), F32),
            pltpu.SemaphoreType.DMA((2 * (src // CHUNK) + 4,)),
        ],
        compiler_params=params(START),
    )(transitions, forward, emission, beta_end, token_ids)


def product_kernel(mine_ref, other_ref, w_ref, v_ref, mul_ref, extra_ref, *rest):
    loads = []
    if len(rest) == 1:
        out_ref, = rest
    else:
        t_hbm, f_hbm, out_ref, t_ref, f_ref, sems = rest
        for i, (source, target) in enumerate(((t_hbm, t_ref), (f_hbm, f_ref))):
            loads.append(pltpu.make_async_copy(source, target, sems.at[i]))
    for c in loads:
        c.start()
    n_chip, rows, _ = out_ref.shape
    piece = rows - EXTRA
    mul = mul_ref[...]
    extra = extra_ref[...]
    group = TILE // piece
    for i in range(n_chip // group):
        at = pl.ds(i * TILE, TILE)
        part = jnp.dot(mine_ref[at, :], w_ref[...], preferred_element_type=F32)
        part = part + jnp.dot(other_ref[at, :], v_ref[...], preferred_element_type=F32)
        part = part * mul
        for j in range(group):
            out_ref[i * group + j, :piece, :] = part[j * piece:(j + 1) * piece]
            out_ref[i * group + j, piece:, :] = extra
    for c in loads:
        c.wait()


def product_call(mine, other, w_own, w_other, mul, extra, n_chip, more):
    rows, seqs = mine.shape[0] // n_chip, w_own.shape[1]
    out = jax.ShapeDtypeStruct((n_chip, rows + EXTRA, seqs), F32)
    return pl.pallas_call(
        product_kernel,
        out_shape=(out,) + tuple(jax.ShapeDtypeStruct(x.shape, x.dtype) for x in more),
        in_specs=[WHOLE] * 6 + [ANY] * len(more),
        out_specs=(WHOLE,) * (1 + len(more)),
        scratch_shapes=[pltpu.SemaphoreType.DMA((2,))] if more else [],
        compiler_params=params(16),
    )(mine, other, w_own, w_other, mul, extra, *more)


def counts_kernel(t_hbm, f_hbm, w1_ref, w0_ref, raw_ref, sums_ref, out_hbm, beta_ref, log_ref,
                  t_ref, f_ref, o_ref, w1t_ref, w0t_ref, sems):
    src, seqs = f_ref.shape[1:]
    parts = src // TILE
    loads, stores = [], []
    for i in range(parts):
        rows = pl.ds(i * TILE, TILE)
        loads.append((
            pltpu.make_async_copy(f_hbm.at[:, rows, :], f_ref.at[:, rows, :], sems.at[3 * i]),
            pltpu.make_async_copy(t_hbm.at[rows, :], t_ref.at[rows, :], sems.at[3 * i + 1]),
        ))
        stores.append(pltpu.make_async_copy(o_ref.at[rows, :], out_hbm.at[rows, :], sems.at[3 * i + 2]))
        for c in loads[i]:
            c.start()
    w1t_ref[...] = w1_ref[...].T
    w0t_ref[...] = w0_ref[...].T
    beta_ref[...] = raw_ref[...] / sums_ref[2:3, :]
    log_ref[...] = jnp.log(sums_ref[2:4, :])
    inv = (1.0 / seqs) / sums_ref[0:2, :]
    for i in range(parts):
        for c in loads[i]:
            c.wait()
        at = slice(i * TILE, (i + 1) * TILE)
        post1 = (f_ref[1, at, :].astype(F32) * inv[1:2]).astype(BF16)
        post0 = (f_ref[0, at, :].astype(F32) * inv[0:1]).astype(BF16)
        mixed = jnp.dot(post1, w1t_ref[...], preferred_element_type=F32)
        mixed = mixed + jnp.dot(post0, w0t_ref[...], preferred_element_type=F32)
        o_ref[at, :] = t_ref[at, :].astype(F32) * mixed
        stores[i].start()
    for c in stores:
        c.wait()


def counts_call(transitions, forward, w1, w0, raw, sums):
    src, dst = transitions.shape
    steps, _, seqs = forward.shape
    return pl.pallas_call(
        counts_kernel,
        out_shape=(
            jax.ShapeDtypeStruct((src, dst), F32),
            jax.ShapeDtypeStruct(raw.shape, F32),
            jax.ShapeDtypeStruct((steps, seqs), F32),
        ),
        in_specs=[ANY] * 2 + [WHOLE] * 4,
        out_specs=(ANY, WHOLE, WHOLE),
        scratch_shapes=[
            pltpu.VMEM((src, dst), BF16),
            pltpu.VMEM((steps, src, seqs), BF16),
            pltpu.VMEM((src, dst), F32),
            pltpu.VMEM((seqs, dst), BF16),
            pltpu.VMEM((seqs, dst), BF16),
            pltpu.SemaphoreType.DMA((3 * (src // TILE),)),
        ],
        compiler_params=params(COUNTS),
    )(transitions, forward, w1, w0, raw, sums)


def local(transitions, forward, emission, beta_end, token_ids):
    src, dst = transitions.shape
    piece, seqs = beta_end.shape
    n_row = lax.axis_size("row")
    n_chip = lax.axis_size("y") * lax.axis_size("x")
    n_core = lax.axis_size("core")
    states = float(dst * n_chip * n_core)
    core = lax.axis_index("core")
    swap = [(i, (i + 1) % n_core) for i in range(n_core)]

    def spread(rows):
        return jnp.broadcast_to(rows[None], (n_row,) + rows.shape)

    chunks = transitions.reshape(n_chip, n_core, piece, dst)
    theirs = lax.dynamic_index_in_dim(chunks, 1 - core, 1, keepdims=False).reshape(src // 2, dst)
    t_other = lax.ppermute(theirs, "core", swap)
    pay, mine, alpha, observed = start_call(
        transitions, forward, emission, beta_end, token_ids, n_row
    )
    pay, mine, t_other = lax.optimization_barrier((pay, mine, t_other))

    block = lax.all_to_all(pay, "row", 0, 0)
    w1 = block[:, :piece].reshape(dst, seqs)
    g_own = jnp.sum(block[:, piece:2 * piece].astype(F32), axis=0)
    cs = jnp.sum(block[:, 2 * piece:2 * piece + 3].astype(F32), axis=(0, 1))
    cs = jnp.stack(split3(cs))

    def backward(w_own, totals, more=()):
        w_other = lax.ppermute(w_own, "core", swap)
        sc = jnp.sum(jnp.dot(cs, w_own, preferred_element_type=F32), axis=0) / states / states
        own = jnp.stack([sc] + totals)
        both = own + lax.ppermute(own, "core", swap)
        power = jnp.ceil(jnp.log2(both[0]))
        down = jnp.exp2(-power)
        rows = [power]
        for i in range(both.shape[0]):
            rows += split2(both[i] * down)
        mul = (down / states)[None, :]
        data, *near = product_call(mine, t_other, w_own, w_other, mul, rows8(rows), n_chip, more)
        return data.astype(F16), both.shape[0], near

    def collect(data, n):
        got = lax.all_to_all(data, CHIPS, 0, 0).astype(F32)
        up = jnp.exp2(got[:, piece:piece + 1])
        raw = jnp.sum(got[:, :piece] * up, axis=0)
        sums = jnp.sum(got[:, piece + 1:] * up, axis=0)
        return raw, [sums[2 * i] + sums[2 * i + 1] for i in range(n)]

    data, n, _ = backward(w1, [])
    data, g_own = lax.optimization_barrier((data, g_own))
    raw, (scale1,) = collect(data, n)

    weights = (observed * (raw / scale1[None, :])).astype(BF16)
    norm1 = jnp.sum(alpha * raw, axis=0) / states
    norm0 = jnp.sum(weights.astype(F32) * g_own, axis=0) / states / states
    pay = jnp.concatenate([weights, rows8(split3(norm1) + split3(norm0))], axis=0)
    block = lax.all_to_all(spread(pay), "row", 0, 0)
    w0 = block[:, :piece].reshape(dst, seqs)
    sums = jnp.sum(block[:, piece:].astype(F32), axis=0)
    norm1 = sums[0] + sums[1] + sums[2]
    norm0 = sums[3] + sums[4] + sums[5]
    data, n, _ = backward(w0, [norm1, norm0])
    raw, (scale0, norm1, norm0) = collect(data, n)

    sums = rows8([norm0, norm1, scale0, scale1])
    return counts_call(transitions, forward, w1, w0, raw, sums)


def solution(mesh):
    n_row, n_col = mesh.devices.shape
    grid = Mesh(mesh.devices.reshape(n_row, 4, n_col // 8, 2), ("row",) + COL)
    in_specs = (
        P("row", COL),
        P(None, "row", None),
        P(None, ("row",) + COL, None),
        P(("row",) + COL, None),
        P(),
    )
    out_specs = (P("row", COL), P(("row",) + COL, None), P())
    return jax.shard_map(local, mesh=grid, in_specs=in_specs, out_specs=out_specs, check_vma=False)
```

```python
import jax
import jax.numpy as jnp
from jax import lax
from jax.experimental import pallas as pl
from jax.experimental.pallas import tpu as pltpu
from jax.sharding import Mesh, PartitionSpec as P

VOCAB = 50257
COL = ("y", "x", "core")
CHIPS = ("y", "x")
BF16 = jnp.bfloat16
F16 = jnp.float16
F32 = jnp.float32
EXTRA = 8
TILE = 256
CHUNK = 512
START = 50
ROWS = 512
COUNTS = 52
ANY = pl.BlockSpec(memory_space=pl.ANY)
NT = (((1,), (1,)), ((), ()))
TN = (((0,), (0,)), ((), ()))
WHOLE = pl.BlockSpec(memory_space=pltpu.VMEM)


def params(mib):
    return pltpu.CompilerParams(vmem_limit_bytes=mib * 1024 * 1024)


def split3(v):
    hi = lax.reduce_precision(v, 8, 7)
    mid = lax.reduce_precision(v - hi, 8, 7)
    return [part.astype(BF16) for part in (hi, mid, v - hi - mid)]


def split2(v):
    hi = lax.reduce_precision(v, 5, 10)
    return [hi, lax.reduce_precision(v - hi, 5, 10)]


def rows8(rows):
    block = jnp.stack(rows)
    return jnp.pad(block, ((0, EXTRA - block.shape[0]), (0, 0)))


def column():
    core = lax.axis_index("core")
    chip = lax.axis_index("y") * lax.axis_size("x") + lax.axis_index("x")
    return core, chip * lax.axis_size("core") + core


def start_kernel(t_hbm, f_hbm, e_hbm, b_hbm, tok_hbm, pay_ref, mine_ref, alpha_ref, seen_ref,
                 t_ref, f_ref, a_ref, e_ref, b_ref, tok_ref, g_ref, sems):
    core, col = column()
    piece = b_ref.shape[0]
    src = t_ref.shape[0]
    parts = src // CHUNK

    def copy(source, target, i):
        c = pltpu.make_async_copy(source, target, sems.at[i])
        c.start()
        return c

    loads = []
    for i in range(parts):
        rows = pl.ds(i * CHUNK, CHUNK)
        loads.append((
            copy(t_hbm.at[rows, :], t_ref.at[rows, :], 2 * i),
            copy(f_hbm.at[0, rows, :], f_ref.at[rows, :], 2 * i + 1),
        ))
    own = pl.ds(pl.multiple_of(col * piece, piece), piece)
    small = [
        copy(f_hbm.at[1, own, :], a_ref, 2 * parts),
        copy(e_hbm, e_ref, 2 * parts + 1),
        copy(b_hbm, b_ref, 2 * parts + 2),
        copy(tok_hbm, tok_ref, 2 * parts + 3),
    ]
    ones = jnp.ones((EXTRA, CHUNK), BF16)
    sums = jnp.zeros((EXTRA, t_ref.shape[1]), F32)
    for i in range(parts):
        for c in loads[i]:
            c.wait()
        t = t_ref[i * CHUNK:(i + 1) * CHUNK, :]
        f = f_ref[i * CHUNK:(i + 1) * CHUNK, :]
        g = lax.dot_general(t, f, TN, preferred_element_type=F32)
        if i == 0:
            g_ref[...] = g
        else:
            g_ref[...] += g
        sums = sums + jnp.dot(ones, t, preferred_element_type=F32)
    for i in range(src // (2 * piece)):
        rows = pl.ds(pl.multiple_of((2 * i + core) * piece, piece), piece)
        mine_ref[i * piece:(i + 1) * piece, :] = t_ref[rows, :]
    for c in small:
        c.wait()
    alpha_ref[...] = a_ref[...].astype(F32)
    ended = tok_ref[...] == VOCAB - 1
    seen_ref[...] = jnp.where(ended[0:1], F32(1.0), e_ref[0].astype(F32))
    observed = jnp.where(ended[1:2], F32(1.0), e_ref[1].astype(F32))
    weights = (observed * b_ref[...]).astype(BF16)
    hi = sums.astype(BF16).astype(F32)
    mid = (sums - hi).astype(BF16).astype(F32)
    lo = sums - hi - mid
    row = lax.broadcasted_iota(jnp.int32, sums.shape, 0)
    tail = jnp.where(row == 0, hi, jnp.where(row == 1, mid, jnp.where(row == 2, lo, F32(0.0))))
    tail = tail.astype(BF16)
    for r in range(pay_ref.shape[0]):
        part = g_ref[r * piece:(r + 1) * piece, :].astype(BF16)
        pay_ref[r] = jnp.concatenate([weights, part, tail], axis=0)


def start_call(transitions, forward, emission, beta_end, token_ids, n_row):
    src, dst = transitions.shape
    piece, seqs = beta_end.shape
    return pl.pallas_call(
        start_kernel,
        out_shape=(
            jax.ShapeDtypeStruct((n_row, 2 * piece + EXTRA, seqs), BF16),
            jax.ShapeDtypeStruct((src // 2, dst), BF16),
            jax.ShapeDtypeStruct((piece, seqs), F32),
            jax.ShapeDtypeStruct((piece, seqs), F32),
        ),
        in_specs=[pl.BlockSpec(memory_space=pl.ANY)] * 5,
        out_specs=(WHOLE,) * 4,
        scratch_shapes=[
            pltpu.VMEM((src, dst), BF16),
            pltpu.VMEM((src, seqs), BF16),
            pltpu.VMEM((piece, seqs), BF16),
            pltpu.VMEM(emission.shape, BF16),
            pltpu.VMEM((piece, seqs), F32),
            pltpu.VMEM(token_ids.shape, jnp.int32),
            pltpu.VMEM((dst, seqs), F32),
            pltpu.SemaphoreType.DMA((2 * (src // CHUNK) + 4,)),
        ],
        compiler_params=params(START),
    )(transitions, forward, emission, beta_end, token_ids)


def product_kernel(mine_ref, other_ref, w_ref, v_ref, mul_ref, extra_ref, *rest):
    loads = []
    if len(rest) == 1:
        out_ref, = rest
    else:
        t_hbm, f_hbm, out_ref, t_ref, f_ref, sems = rest
        for i, (source, target) in enumerate(((t_hbm, t_ref), (f_hbm, f_ref))):
            loads.append(pltpu.make_async_copy(source, target, sems.at[i]))
    for c in loads:
        c.start()
    n_chip, rows, _ = out_ref.shape
    piece = rows - EXTRA
    mul = mul_ref[...]
    extra = extra_ref[...]
    group = TILE // piece
    for i in range(n_chip // group):
        at = pl.ds(i * TILE, TILE)
        part = jnp.dot(mine_ref[at, :], w_ref[...], preferred_element_type=F32)
        part = part + jnp.dot(other_ref[at, :], v_ref[...], preferred_element_type=F32)
        part = part * mul
        for j in range(group):
            out_ref[i * group + j, :piece, :] = part[j * piece:(j + 1) * piece]
            out_ref[i * group + j, piece:, :] = extra
    for c in loads:
        c.wait()


def product_call(mine, other, w_own, w_other, mul, extra, n_chip, more):
    rows, seqs = mine.shape[0] // n_chip, w_own.shape[1]
    out = jax.ShapeDtypeStruct((n_chip, rows + EXTRA, seqs), F32)
    return pl.pallas_call(
        product_kernel,
        out_shape=(out,) + tuple(jax.ShapeDtypeStruct(x.shape, x.dtype) for x in more),
        in_specs=[WHOLE] * 6 + [ANY] * len(more),
        out_specs=(WHOLE,) * (1 + len(more)),
        scratch_shapes=[pltpu.SemaphoreType.DMA((2,))] if more else [],
        compiler_params=params(16),
    )(mine, other, w_own, w_other, mul, extra, *more)


def counts_kernel(t_hbm, f_hbm, w1_ref, w0_ref, raw_ref, sums_ref, out_hbm, beta_ref, log_ref,
                  t_ref, f_ref, o_ref, sems):
    src, seqs = f_ref.shape[1:]
    parts = src // ROWS
    loads, stores = [], []
    for i in range(parts):
        rows = pl.ds(i * ROWS, ROWS)
        loads.append((
            pltpu.make_async_copy(f_hbm.at[:, rows, :], f_ref.at[:, rows, :], sems.at[3 * i]),
            pltpu.make_async_copy(t_hbm.at[rows, :], t_ref.at[rows, :], sems.at[3 * i + 1]),
        ))
        stores.append(pltpu.make_async_copy(o_ref.at[rows, :], out_hbm.at[rows, :], sems.at[3 * i + 2]))
        for c in loads[i]:
            c.start()
    beta_ref[...] = raw_ref[...] / sums_ref[2:3, :]
    log_ref[...] = jnp.log(sums_ref[2:4, :])
    inv = (1.0 / seqs) / sums_ref[0:2, :]
    for i in range(parts):
        for c in loads[i]:
            c.wait()
        at = slice(i * ROWS, (i + 1) * ROWS)
        post1 = (f_ref[1, at, :].astype(F32) * inv[1:2]).astype(BF16)
        post0 = (f_ref[0, at, :].astype(F32) * inv[0:1]).astype(BF16)
        mixed = lax.dot_general(post1, w1_ref[...], NT, preferred_element_type=F32)
        mixed = mixed + lax.dot_general(post0, w0_ref[...], NT, preferred_element_type=F32)
        o_ref[at, :] = t_ref[at, :].astype(F32) * mixed
        stores[i].start()
    for c in stores:
        c.wait()


def counts_call(transitions, forward, w1, w0, raw, sums):
    src, dst = transitions.shape
    steps, _, seqs = forward.shape
    return pl.pallas_call(
        counts_kernel,
        out_shape=(
            jax.ShapeDtypeStruct((src, dst), F32),
            jax.ShapeDtypeStruct(raw.shape, F32),
            jax.ShapeDtypeStruct((steps, seqs), F32),
        ),
        in_specs=[ANY] * 2 + [WHOLE] * 4,
        out_specs=(ANY, WHOLE, WHOLE),
        scratch_shapes=[
            pltpu.VMEM((src, dst), BF16),
            pltpu.VMEM((steps, src, seqs), BF16),
            pltpu.VMEM((src, dst), F32),
            pltpu.SemaphoreType.DMA((3 * (src // ROWS),)),
        ],
        compiler_params=params(COUNTS),
    )(transitions, forward, w1, w0, raw, sums)


def local(transitions, forward, emission, beta_end, token_ids):
    src, dst = transitions.shape
    piece, seqs = beta_end.shape
    n_row = lax.axis_size("row")
    n_chip = lax.axis_size("y") * lax.axis_size("x")
    n_core = lax.axis_size("core")
    states = float(dst * n_chip * n_core)
    core = lax.axis_index("core")
    swap = [(i, (i + 1) % n_core) for i in range(n_core)]

    def spread(rows):
        return jnp.broadcast_to(rows[None], (n_row,) + rows.shape)

    chunks = transitions.reshape(n_chip, n_core, piece, dst)
    theirs = lax.dynamic_index_in_dim(chunks, 1 - core, 1, keepdims=False).reshape(src // 2, dst)
    t_other = lax.ppermute(theirs, "core", swap)
    pay, mine, alpha, observed = start_call(
        transitions, forward, emission, beta_end, token_ids, n_row
    )
    pay, mine, t_other = lax.optimization_barrier((pay, mine, t_other))

    block = lax.all_to_all(pay, "row", 0, 0)
    w1 = block[:, :piece].reshape(dst, seqs)
    g_own = jnp.sum(block[:, piece:2 * piece].astype(F32), axis=0)
    cs = jnp.sum(block[:, 2 * piece:2 * piece + 3].astype(F32), axis=(0, 1))
    cs = jnp.stack(split3(cs))

    def backward(w_own, totals, more=()):
        w_other = lax.ppermute(w_own, "core", swap)
        sc = jnp.sum(jnp.dot(cs, w_own, preferred_element_type=F32), axis=0) / states / states
        own = jnp.stack([sc] + totals)
        both = own + lax.ppermute(own, "core", swap)
        power = jnp.ceil(jnp.log2(both[0]))
        down = jnp.exp2(-power)
        rows = [power]
        for i in range(both.shape[0]):
            rows += split2(both[i] * down)
        mul = (down / states)[None, :]
        data, *near = product_call(mine, t_other, w_own, w_other, mul, rows8(rows), n_chip, more)
        return data.astype(F16), both.shape[0], near

    def collect(data, n):
        got = lax.all_to_all(data, CHIPS, 0, 0).astype(F32)
        up = jnp.exp2(got[:, piece:piece + 1])
        raw = jnp.sum(got[:, :piece] * up, axis=0)
        sums = jnp.sum(got[:, piece + 1:] * up, axis=0)
        return raw, [sums[2 * i] + sums[2 * i + 1] for i in range(n)]

    data, n, _ = backward(w1, [])
    data, g_own = lax.optimization_barrier((data, g_own))
    raw, (scale1,) = collect(data, n)

    weights = (observed * (raw / scale1[None, :])).astype(BF16)
    norm1 = jnp.sum(alpha * raw, axis=0) / states
    norm0 = jnp.sum(weights.astype(F32) * g_own, axis=0) / states / states
    pay = jnp.concatenate([weights, rows8(split3(norm1) + split3(norm0))], axis=0)
    block = lax.all_to_all(spread(pay), "row", 0, 0)
    w0 = block[:, :piece].reshape(dst, seqs)
    sums = jnp.sum(block[:, piece:].astype(F32), axis=0)
    norm1 = sums[0] + sums[1] + sums[2]
    norm0 = sums[3] + sums[4] + sums[5]
    data, n, _ = backward(w0, [norm1, norm0])
    raw, (scale0, norm1, norm0) = collect(data, n)

    sums = rows8([norm0, norm1, scale0, scale1])
    return counts_call(transitions, forward, w1, w0, raw, sums)


def solution(mesh):
    n_row, n_col = mesh.devices.shape
    grid = Mesh(mesh.devices.reshape(n_row, 4, n_col // 8, 2), ("row",) + COL)
    in_specs = (
        P("row", COL),
        P(None, "row", None),
        P(None, ("row",) + COL, None),
        P(("row",) + COL, None),
        P(),
    )
    out_specs = (P("row", COL), P(("row",) + COL, None), P())
    return jax.shard_map(local, mesh=grid, in_specs=in_specs, out_specs=out_specs, check_vma=False)
```
